32 devices in a mesh: sec: 4 (over y, x), row: 8 (over z, core).
Axes of the slice: x: 2, y: 2, z: 4, core: 2. Of those that a mesh axis runs over, the one named last changes fastest.
Arguments:
- rhs: float32 [4096, 256], P(('sec', 'row')), may hold values from -6 to 6
- coupling: bfloat16 [4, 1024, 4096], P(None, 'row', 'sec'), may hold values from -0.09375 to 0.09375
- diag_inverse: bfloat16 [4, 1024, 1024], P('sec'), as said below
Outputs:
- solution: float32 [4096, 256], P(('sec', 'row'))
- forward: float32 [4096, 256], P(('sec', 'row'))
The draws below stay inside these ranges and needn't reach their ends.
Inputs may be any that keep to these rules, and one draw needn't show every extreme that they name: `diag_inverse`: each of the 4 blocks is lower triangular with diagonal entries from 0.5 to 1.5.
All inputs are finite; a program needn't handle non-finite values.
Results may differ from the reference program's by a relative error of at most 0.02.
Values may be sent and summed in bfloat16 or wider, within the bound.
A program may use at most 64 MiB of HBM per device.

```python
import jax
import jax.numpy as jnp
from jax import lax

W = 1024
SECTIONS = 4
M = 4096
NRHS = 256
N_ROW = 8


def draw_diag_inverse(key, part):
    base = jax.random.fold_in(key, 11)
    first, second = jax.random.split(base)
    index = jnp.arange(W)
    lower = index[:, None] > index[None, :]
    below = jax.random.normal(first, (SECTIONS, W, W), jnp.float32) * (0.5 / W ** 0.5)
    diagonal = jnp.exp(jax.random.uniform(second, (SECTIONS, W), jnp.float32, jnp.log(0.5), jnp.log(1.5)))
    eye = (index[:, None] == index[None, :]).astype(jnp.float32)
    result = jnp.where(lower[None], below, 0.0) + eye[None] * diagonal[:, :, None]
    return result.astype(jnp.bfloat16)


def block_scale(key, extent, shards, smallest, high):
    loudness = 1.0
    for position, blocks in shards:
        heights = jax.random.uniform(jax.random.fold_in(jax.random.fold_in(key, 6), position), (blocks,), jnp.float32, smallest / len(shards), high / len(shards))
        loudness = loudness * jnp.repeat(jnp.exp(heights), extent[position] // blocks).reshape((-1,) + (1,) * (len(extent) - 1 - position))
    return loudness


def noise(key, extent, scale, bound, shards=(), dtype=jnp.bfloat16):
    level = block_scale(key, extent, shards, -0.22, 0.18) if shards else 1.0
    drawn = jax.random.normal(key, extent, jnp.float32) * scale * level
    return jnp.minimum(jnp.maximum(drawn, -bound), bound).astype(dtype)


def setup_inputs(seed: int = 0) -> dict:
    streams_of = jax.random.split(jax.random.key(seed), 4)
    return {
        "rhs": noise(streams_of[0], (M, NRHS), 1.0, 6.0, ((0, 32),), jnp.float32),
        "coupling": noise(streams_of[1], (SECTIONS, W, M), M ** -0.5, 0.09375, ((1, 8), (2, 4))),
        "diag_inverse": draw_diag_inverse(jax.random.fold_in(streams_of[3], 71), 0),
    }


def reference(rhs, coupling, diag_inverse):
    sections = SECTIONS
    width = W
    rows = W // N_ROW
    forward_parts = []
    low_forward = []
    for sec_now in range(sections):
        accum = jnp.zeros((width, NRHS), jnp.float32)
        for earlier in range(sec_now):
            block = coupling[sec_now, :, earlier * width:(earlier + 1) * width]
            accum = accum + jnp.dot(block, low_forward[earlier], preferred_element_type=jnp.float32)
        resid = (rhs[sec_now * width:(sec_now + 1) * width] - accum).astype(jnp.bfloat16)
        solved = jnp.dot(diag_inverse[sec_now], resid, preferred_element_type=jnp.float32)
        forward_parts.append(solved)
        low_forward.append(solved.astype(jnp.bfloat16))
    low_solution = [None] * sections
    solution_parts = [None] * sections
    for sec_now in range(sections - 1, -1, -1):
        partial_value = jnp.zeros((N_ROW, width, NRHS), jnp.float32)
        for later in range(sec_now + 1, sections):
            block = coupling[later, :, sec_now * width:(sec_now + 1) * width].astype(jnp.float32)
            block = block.reshape(N_ROW, rows, width)
            solved_later = low_solution[later].astype(jnp.float32).reshape(N_ROW, rows, NRHS)
            partial_value = partial_value + jnp.einsum('gjw,gjc->gwc', block, solved_later)
        rounded = lax.optimization_barrier(partial_value.astype(jnp.bfloat16))
        summed = jnp.sum(rounded.astype(jnp.float32), axis=0)
        lowered = (forward_parts[sec_now] - summed).astype(jnp.bfloat16)
        solved = lax.dot_general(diag_inverse[sec_now], lowered, (((0,), (0,)), ((), ())), preferred_element_type=jnp.float32)
        solution_parts[sec_now] = solved
        low_solution[sec_now] = solved.astype(jnp.bfloat16)
    return jnp.concatenate(solution_parts, axis=0), jnp.concatenate(forward_parts, axis=0)
```

```python
import functools

import jax
import jax.numpy as jnp
from jax import lax
from jax.experimental import pallas as pl
from jax.experimental.pallas import tpu as pltpu
from jax.sharding import PartitionSpec as P

MESH = pl.DeviceIdType.MESH
F32 = jnp.float32
BF16 = jnp.bfloat16
GROUPS = 4


def nt(a, b):
    return lax.dot_general(a, b, (((1,), (1,)), ((), ())), preferred_element_type=F32)


def nn(a, b):
    return jnp.dot(a, b, preferred_element_type=F32)


def kernel(S, R, G, rhs, coup, D, sol, fwd,
           E, rT, rTl, rb, res, mco, pas, pso, yb, fs, fb, dto, dti, xs, rso, rsi, rli, sob, soi,
           e_s, e_r, rh_s, rh_r, a0_s, a0_r, mc_s, mc_r, ps_s, ps_r, dt_s, dt_r,
           xs_s, xs_r, rs_s, rs_r, rl_r, so_s, so_r, fo_s, fo_r):
    sec = lax.axis_index("sec")
    row = lax.axis_index("row")
    z, c = row // 2, row % 2
    Z = R // 2
    rows, total = rhs.shape
    W = D.shape[0]
    N = total // 2
    n = N // G
    RZ = 2 * rows

    def rc(src, dst, ss, rs, dsec, drow):
        return pltpu.make_async_remote_copy(
            src_ref=src, dst_ref=dst, send_sem=ss, recv_sem=rs,
            device_id=(dsec, drow), device_id_type=MESH)

    barrier = pltpu.get_barrier_semaphore()

    def signal(dsec, drow):
        pl.semaphore_signal(barrier, inc=1, device_id=(dsec, drow), device_id_type=MESH)

    for k in range(1, R):
        signal(sec, lax.rem(row + k, R))
    for ds in (-1, 1):
        ok = (sec + ds >= 0) & (sec + ds < S)

        @pl.when(ok)
        def _(ds=ds):
            for q in range(Z):
                signal(sec + ds, 2 * q + c)
            signal(sec + ds, 2 * z + 1 - c)

    for k in range(2):
        t = rhs[:, k * N:(k + 1) * N].T.reshape(G, n, rows)
        rT[k] = t
        rTl[k] = t.astype(BF16)

    sides = jnp.where(sec > 0, 1, 0) + jnp.where(sec < S - 1, 1, 0)
    pl.semaphore_wait(barrier, R - 1 + sides * (Z + 1))

    def a0(k):
        to = lax.rem(row + k, R)
        return rc(rTl.at[to % 2], res.at[row], a0_s.at[k], a0_r.at[k], sec, to)

    def rh(k):
        return rc(rT.at[k], rb.at[c], rh_s.at[k], rh_r.at[c], sec - 1, 2 * z + k)

    @pl.when(sec == 0)
    def _():
        for k in range(1, R):
            a0(k).start()
        res[row] = rTl[c]

    @pl.when(sec > 0)
    def _():
        for k in range(2):
            rh(k).start()

    mine = pl.ds(pl.multiple_of(c * rows, rows), rows)

    def ex(t):
        return rc(E.at[t, mine], E.at[t, mine], e_s.at[t], e_r.at[t], sec, 2 * z + 1 - c)

    def make(t, _):
        E[t, mine] = nn(coup[t], D[...]).astype(BF16)
        ex(t).start()
        return 0

    lax.fori_loop(sec + 1, S, make, 0)

    def gathered(g):
        return jnp.concatenate([res[r, g] for r in range(R)], axis=1)

    def mc(s, g, q):
        to = lax.rem(z + q, Z)
        return rc(mco.at[g], res.at[pl.ds(2 * z, 2), g], mc_s.at[g, q], mc_r.at[g, q],
                  s + 1, 2 * to + c)

    def ps(s, t, g):
        return rc(pso.at[t, g], pas.at[t, g], ps_s.at[t, g], ps_r.at[t, g], s + 1, row)

    def xp(s, t, g):
        return rc(xs.at[t, g], xs.at[t, g], xs_s.at[t, g], xs_r.at[t, g], s - 1, row)

    def rsc(s, g, q):
        to = lax.rem(z + q, Z)
        return rc(rso.at[to, g], rsi.at[z, g], rs_s.at[g, q], rs_r.at[g, q],
                  s - 1, 2 * to + c)

    def rlc(g, q):
        to = lax.rem(z + q, Z)
        return rc(rso.at[to, g], rli.at[z, g], rs_s.at[g, q], rl_r.at[g, q], sec, 2 * to + c)

    def dt(s):
        return rc(dto, dti, dt_s, dt_r, s - 1, row)

    def fo():
        return rc(fs.at[1 - c], fb.at[c], fo_s, fo_r, sec, 2 * z + 1 - c)

    def so(slot, dsec, h):
        return rc(sob.at[slot, h], soi.at[c], so_s.at[slot, h], so_r.at[c], dsec, 2 * z + h)

    def own_columns(low):
        if RZ % 128 == 0:
            v = nn(low, D[:, pl.ds(pl.multiple_of(z * RZ, RZ), RZ)])
            return [v[:, :rows], v[:, rows:]]
        v = nn(low, D[...])
        out = [jnp.zeros((low.shape[0], rows), F32) for _ in range(2)]
        for r in range(R):
            out[r % 2] = jnp.where(z == r // 2, v[:, r * rows:(r + 1) * rows], out[r % 2])
        return out

    def section(s):
        last = s == S - 1

        if s == 0:
            for k in range(1, R):
                to = lax.rem(row + R - k, R)
                rc(rTl.at[0], res.at[to], a0_s.at[k], a0_r.at[k], sec, to).wait_recv()
        if not last:
            for k in range(2):
                rc(rT.at[k], rb.at[k], rh_s.at[k], rh_r.at[k], sec, row).wait_recv()
            for t in range(s + 1, S):
                other = pl.ds(pl.multiple_of((1 - c) * rows, rows), rows)
                rc(E.at[t, other], E.at[t, other], e_s.at[t], e_r.at[t], sec, row).wait_recv()

        def forward(g, _):
            if s > 0:
                for q in range(Z):
                    src = lax.rem(z + Z - q, Z)
                    rc(mco.at[g], res.at[pl.ds(2 * src, 2), g], mc_s.at[g, q], mc_r.at[g, q],
                       sec, row).wait_recv()
            x = gathered(g)
            if last:
                y = nt(x, D[...])
                for r in range(R):
                    yb[r, g] = y[:, r * rows:(r + 1) * rows]
                v = own_columns(y.astype(BF16))
                for h in range(2):
                    sob[0, h, g] = v[h]
                    xs[s, g, h] = v[h].astype(BF16)
                xp(s, s, g).start()
                return 0
            for t in range(s + 1, S):
                a = nt(x, E[t])
                if s > 0:
                    ps(s, t, g).wait_recv()
                for h in range(2):
                    ah = a[:, h * rows:(h + 1) * rows]
                    if s > 0:
                        ah = ah + pas[t, g, h].astype(F32)
                    if t == s + 1:
                        mco[g, h] = (rb[h, g] - ah).astype(BF16)
                    else:
                        pso[t, g, h] = ah.astype(BF16)
                if t == s + 1:
                    for q in range(Z):
                        mc(s, g, q).start()
                else:
                    ps(s, t, g).start()
            return 0

        lax.fori_loop(0, G, forward, 0)

        if not last:
            x = jnp.concatenate([res[r].reshape(N, rows) for r in range(R)], axis=1)
            y = nt(x, D[...])
            for r in range(R):
                yb[r] = y[:, r * rows:(r + 1) * rows].reshape(G, n, rows)
            v = own_columns(y.astype(BF16))
            for h in range(2):
                dto[h] = v[h].reshape(G, n, rows)
            if s > 0:
                dt(s).start()
        fs[...] = yb[pl.ds(2 * z, 2)]
        fo().start()
        fb[c] = fs[c]

        if last:
            so(0, s, 1 - c).start()
            soi[c] = sob[0, c]
        else:
            if s < S - 2:
                rc(dto, dti, dt_s, dt_r, sec, row).wait_recv()

            def backward(g, _):
                for t in range(S - 1, s, -1):
                    if t > s + 1 or t == S - 1:
                        xp(s + 1, t, g).wait_recv()
                    else:
                        v = [dti[h, g] for h in range(2)]
                        for q in range(Z):
                            src = lax.rem(z + Z - q, Z)
                            rc(rso.at[0, g], rsi.at[src, g], rs_s.at[g, q], rs_r.at[g, q],
                               sec, row).wait_recv()
                            v = [v[h] - rsi[src, g, h].astype(F32) for h in range(2)]
                        for h in range(2):
                            sob[0, h, g] = v[h]
                            xs[t, g, h] = v[h].astype(BF16)
                    term = nn(jnp.concatenate([xs[t, g, 0], xs[t, g, 1]], axis=1), E[t])
                    p = term if t == S - 1 else p + term
                for r in range(R):
                    rso[r // 2, g, r % 2] = p[:, r * rows:(r + 1) * rows].astype(BF16)
                for q in range(Z):
                    if s > 0:
                        rsc(s, g, q).start()
                    elif q > 0:
                        rlc(g, q).start()
                if s > 0:
                    for t in range(s + 1, S):
                        xp(s, t, g).start()
                return 0

            lax.fori_loop(0, G, backward, 0)
            if s < S - 2:
                for h in range(2):
                    so(0, s + 1, h).start()
            if s == 0:
                def finish(g, _):
                    v = [dto[h, g] - rso[z, g, h].astype(F32) for h in range(2)]
                    for q in range(1, Z):
                        src = lax.rem(z + Z - q, Z)
                        rc(rso.at[0, g], rli.at[src, g], rs_s.at[g, q], rl_r.at[g, q],
                           sec, row).wait_recv()
                        v = [v[h] - rli[src, g, h].astype(F32) for h in range(2)]
                    for h in range(2):
                        sob[1, h, g] = v[h]
                    return 0

                lax.fori_loop(0, G, finish, 0)
                so(1, s, 1 - c).start()
                soi[c] = sob[1, c]

        rc(fs.at[0], fb.at[1 - c], fo_s, fo_r, sec, row).wait_recv()
        fwd[...] = jnp.concatenate([fb[k].reshape(N, rows).T for k in range(2)], axis=1)
        if s == 0 or last:
            rc(sob.at[0, 0], soi.at[1 - c], so_s.at[0, 0], so_r.at[1 - c], sec, row).wait_recv()
        else:
            for k in range(2):
                rc(sob.at[0, 0], soi.at[k], so_s.at[0, 0], so_r.at[k], sec, row).wait_recv()
        sol[...] = jnp.concatenate([soi[k].reshape(N, rows).T for k in range(2)], axis=1)

        if s == 0:
            for k in range(1, R):
                a0(k).wait_send()
        else:
            for k in range(2):
                rh(k).wait_send()
        for t in range(s + 1, S):
            ex(t).wait_send()
        fo().wait_send()
        if 0 < s < S - 1:
            dt(s).wait_send()

        def drain(g, _):
            if not last:
                for q in range(Z):
                    mc(s, g, q).wait_send()
                    if s > 0:
                        rsc(s, g, q).wait_send()
                    elif q > 0:
                        rlc(g, q).wait_send()
                for t in range(s + 2, S):
                    ps(s, t, g).wait_send()
            if s > 0:
                for t in range(min(s + 1, S - 1), S):
                    xp(s, t, g).wait_send()
            return 0

        lax.fori_loop(0, G, drain, 0)
        if last:
            so(0, s, 1 - c).wait_send()
        elif s < S - 2:
            for h in range(2):
                so(0, s + 1, h).wait_send()
        if s == 0:
            so(1, s, 1 - c).wait_send()

    for s in range(S):
        pl.when(sec == s)(functools.partial(section, s))


def local(rhs, coupling, diag_inverse):
    S = lax.axis_size("sec")
    R = lax.axis_size("row")
    rows, total = rhs.shape
    W = diag_inverse.shape[1]
    N = total // 2
    G = GROUPS
    n = N // G
    Z = R // 2
    half = (G, n, rows)
    vm = pltpu.VMEM
    dma = pltpu.SemaphoreType.DMA
    scratch = [
        vm((S, 2 * rows, W), BF16),
        vm((2,) + half, F32),
        vm((2,) + half, BF16),
        vm((2,) + half, F32),
        vm((R,) + half, BF16),
        vm((G, 2, n, rows), BF16),
        vm((S, G, 2, n, rows), BF16),
        vm((S, G, 2, n, rows), BF16),
        vm((R,) + half, F32),
        vm((2,) + half, F32),
        vm((2,) + half, F32),
        vm((2,) + half, F32),
        vm((2,) + half, F32),
        vm((S, G, 2, n, rows), BF16),
        vm((Z, G, 2, n, rows), BF16),
        vm((Z, G, 2, n, rows), BF16),
        vm((Z, G, 2, n, rows), BF16),
        vm((2, 2) + half, F32),
        vm((2,) + half, F32),
        dma((S,)), dma((S,)),
        dma((2,)), dma((2,)),
        dma((R,)), dma((R,)),
        dma((G, Z)), dma((G, Z)),
        dma((S, G)), dma((S, G)),
        dma, dma,
        dma((S, G)), dma((S, G)),
        dma((G, Z)), dma((G, Z)), dma((G, Z)),
        dma((2, 2)), dma((2,)),
        dma, dma,
    ]
    out = jax.ShapeDtypeStruct((rows, total), F32)
    block = pl.BlockSpec(memory_space=pltpu.VMEM)
    return pl.pallas_call(
        functools.partial(kernel, S, R, G),
        out_shape=(out, out),
        in_specs=[block] * 3,
        out_specs=(block, block),
        scratch_shapes=scratch,
        compiler_params=pltpu.CompilerParams(
            collective_id=0, has_side_effects=True, vmem_limit_bytes=48 * 2 ** 20),
    )(rhs, coupling, diag_inverse[0])


def solution(mesh):
    return jax.shard_map(
        local,
        mesh=mesh,
        in_specs=(P(("sec", "row"), None), P(None, "row", "sec"), P("sec", None, None)),
        out_specs=(P(("sec", "row"), None), P(("sec", "row"), None)),
        check_vma=False,
    )
```

```python
import functools

import jax
import jax.numpy as jnp
from jax import lax
from jax.experimental import pallas as pl
from jax.experimental.pallas import tpu as pltpu
from jax.sharding import PartitionSpec as P

MESH = pl.DeviceIdType.MESH
F32 = jnp.float32
BF16 = jnp.bfloat16
GROUPS = 4


def nt(a, b):
    return lax.dot_general(a, b, (((1,), (1,)), ((), ())), preferred_element_type=F32)


def nn(a, b):
    return jnp.dot(a, b, preferred_element_type=F32)


def kernel(S, R, G, rhs_in, coup_in, D_in, sol, fwd,
           rhs, coup, D, E, rT, rTl, rb, res, mco, pas, pso, yb, fs, fb, dto, xs, rso, rsi, rli, sob, soi,
           in_s, e_s, e_r, rh_s, rh_r, a0_s, a0_r, mc_s, mc_r, ps_s, ps_r,
           xs_s, xs_r, rs_s, rs_r, rl_s, rl_r, so_s, so_r, fo_s, fo_r):
    sec = lax.axis_index("sec")
    row = lax.axis_index("row")
    z, c = row // 2, row % 2
    Z = R // 2
    rows, total = rhs.shape
    W = D.shape[0]
    N = total // 2
    n = N // G
    RZ = 2 * rows

    def rc(src, dst, ss, rs, dsec, drow):
        return pltpu.make_async_remote_copy(
            src_ref=src, dst_ref=dst, send_sem=ss, recv_sem=rs,
            device_id=(dsec, drow), device_id_type=MESH)

    load_rhs = pltpu.make_async_copy(rhs_in, rhs, in_s.at[0])
    load_D = pltpu.make_async_copy(D_in, D, in_s.at[1])
    load_coup = pltpu.make_async_copy(coup_in, coup, in_s.at[2])
    load_rhs.start()
    load_D.start()
    load_coup.start()

    barrier = pltpu.get_barrier_semaphore()

    def signal(dsec, drow):
        pl.semaphore_signal(barrier, inc=1, device_id=(dsec, drow), device_id_type=MESH)

    for k in range(1, R):
        signal(sec, lax.rem(row + k, R))
    for ds in (-1, 1):
        ok = (sec + ds >= 0) & (sec + ds < S)

        @pl.when(ok)
        def _(ds=ds):
            for q in range(Z):
                signal(sec + ds, 2 * q + c)
            signal(sec + ds, 2 * z + 1 - c)

    load_rhs.wait()
    for k in range(2):
        t = rhs[:, k * N:(k + 1) * N].T.reshape(G, n, rows)
        rT[k] = t
        rTl[k] = t.astype(BF16)

    sides = jnp.where(sec > 0, 1, 0) + jnp.where(sec < S - 1, 1, 0)
    pl.semaphore_wait(barrier, R - 1 + sides * (Z + 1))

    def a0(g, k):
        to = lax.rem(row + k, R)
        return rc(rTl.at[to % 2, g], res.at[row, g], a0_s.at[g, k], a0_r.at[g, k], sec, to)

    def rh(k):
        return rc(rT.at[k], rb.at[c], rh_s.at[k], rh_r.at[c], sec - 1, 2 * z + k)

    @pl.when(sec == 0)
    def _():
        def send(g, _):
            for k in range(1, R):
                a0(g, k).start()
            return 0

        lax.fori_loop(0, G, send, 0)
        res[row] = rTl[c]

    @pl.when(sec > 0)
    def _():
        for k in range(2):
            rh(k).start()

    mine = pl.ds(pl.multiple_of(c * rows, rows), rows)

    def ex(t):
        return rc(E.at[t, mine], E.at[t, mine], e_s.at[t], e_r.at[t], sec, 2 * z + 1 - c)

    def make(t, _):
        E[t, mine] = nn(coup[t], D[...]).astype(BF16)
        ex(t).start()
        return 0

    load_D.wait()
    load_coup.wait()
    lax.fori_loop(sec + 1, S, make, 0)

    def gathered(g):
        return jnp.concatenate([res[r, g] for r in range(R)], axis=1)

    def mc(s, g, q):
        to = lax.rem(z + q, Z)
        return rc(mco.at[g], res.at[pl.ds(2 * z, 2), g], mc_s.at[g, q], mc_r.at[g, q],
                  s + 1, 2 * to + c)

    def ps(s, t, g):
        return rc(pso.at[t, g], pas.at[t, g], ps_s.at[t, g], ps_r.at[t, g], s + 1, row)

    def xp(s, t, g):
        return rc(xs.at[t, g], xs.at[t, g], xs_s.at[t, g], xs_r.at[t, g], s - 1, row)

    def rsc(s, g, q):
        to = lax.rem(z + q, Z)
        return rc(rso.at[to, g], rsi.at[z, g], rs_s.at[g, q], rs_r.at[g, q],
                  s - 1, 2 * to + c)

    def rlc(g, k):
        to = lax.rem(row + k, R)
        return rc(rso.at[to // 2, g, to % 2], rli.at[z, c, g], rl_s.at[g, k], rl_r.at[g, k],
                  sec, to)

    def fo():
        return rc(fs.at[1 - c], fb.at[c], fo_s, fo_r, sec, 2 * z + 1 - c)

    def so(slot, dsec, h, g):
        return rc(sob.at[slot, h, g], soi.at[c, g], so_s.at[h, g], so_r.at[c, g], dsec, 2 * z + h)

    def own_columns(low):
        if RZ % 128 == 0:
            v = nn(low, D[:, pl.ds(pl.multiple_of(z * RZ, RZ), RZ)])
            return [v[:, :rows], v[:, rows:]]
        v = nn(low, D[...])
        out = [jnp.zeros((low.shape[0], rows), F32) for _ in range(2)]
        for r in range(R):
            out[r % 2] = jnp.where(z == r // 2, v[:, r * rows:(r + 1) * rows], out[r % 2])
        return out

    def arrived(t):
        other = pl.ds(pl.multiple_of((1 - c) * rows, rows), rows)
        rc(E.at[t, other], E.at[t, other], e_s.at[t], e_r.at[t], sec, row).wait_recv()

    def section(s):
        last = s == S - 1

        if not last:
            for k in range(2):
                rc(rT.at[k], rb.at[k], rh_s.at[k], rh_r.at[k], sec, row).wait_recv()
            arrived(s + 1)

        def forward(g, _):
            if s > 0:
                for q in range(Z):
                    src = lax.rem(z + Z - q, Z)
                    rc(mco.at[g], res.at[pl.ds(2 * src, 2), g], mc_s.at[g, q], mc_r.at[g, q],
                       sec, row).wait_recv()
            else:
                for k in range(1, R):
                    src = lax.rem(row + R - k, R)
                    rc(rTl.at[0, g], res.at[src, g], a0_s.at[g, k], a0_r.at[g, k],
                       sec, row).wait_recv()
            x = gathered(g)
            if last:
                y = nt(x, D[...])
                for r in range(R):
                    yb[r, g] = y[:, r * rows:(r + 1) * rows]
                v = own_columns(y.astype(BF16))
                for h in range(2):
                    sob[0, h, g] = v[h]
                    xs[s, g, h] = v[h].astype(BF16)
                xp(s, s, g).start()
                so(0, s, 1 - c, g).start()
                soi[c, g] = sob[0, c, g]
                return 0
            for t in range(s + 1, S):
                if t > s + 1:
                    pl.when(g == 0)(functools.partial(arrived, t))
                a = nt(x, E[t])
                if s > 0:
                    ps(s, t, g).wait_recv()
                for h in range(2):
                    ah = a[:, h * rows:(h + 1) * rows]
                    if s > 0:
                        ah = ah + pas[t, g, h].astype(F32)
                    if t == s + 1:
                        mco[g, h] = (rb[h, g] - ah).astype(BF16)
                    else:
                        pso[t, g, h] = ah.astype(BF16)
                if t == s + 1:
                    for q in range(Z):
                        mc(s, g, q).start()
                else:
                    ps(s, t, g).start()
            return 0

        lax.fori_loop(0, G, forward, 0)

        if not last:
            x = jnp.concatenate([res[r].reshape(N, rows) for r in range(R)], axis=1)
            y = nt(x, D[...])
            for r in range(R):
                yb[r] = y[:, r * rows:(r + 1) * rows].reshape(G, n, rows)
            v = own_columns(y.astype(BF16))
            for h in range(2):
                dto[h] = v[h].reshape(G, n, rows)
        fs[...] = yb[pl.ds(2 * z, 2)]
        fo().start()
        fb[c] = fs[c]

        if not last:
            def backward(g, _):
                for t in range(S - 1, s, -1):
                    if t > s + 1 or t == S - 1:
                        xp(s + 1, t, g).wait_recv()
                    else:
                        v = [jnp.zeros((n, rows), F32) for h in range(2)]
                        for q in range(Z):
                            src = lax.rem(z + Z - q, Z)
                            rc(rso.at[0, g], rsi.at[src, g], rs_s.at[g, q], rs_r.at[g, q],
                               sec, row).wait_recv()
                            v = [v[h] - rsi[src, g, h].astype(F32) for h in range(2)]
                        for h in range(2):
                            sob[0, h, g] = v[h]
                            xs[t, g, h] = v[h].astype(BF16)
                    term = nn(jnp.concatenate([xs[t, g, 0], xs[t, g, 1]], axis=1), E[t])
                    p = term if t == S - 1 else p + term
                for r in range(R):
                    own = jnp.where(z == r // 2, dto[r % 2, g], 0.0)
                    rso[r // 2, g, r % 2] = (p[:, r * rows:(r + 1) * rows] - own).astype(BF16)
                if s == 0:
                    for k in range(1, R):
                        rlc(g, k).start()
                    rli[z, c, g] = rso[z, g, c]
                else:
                    for q in range(Z):
                        rsc(s, g, q).start()
                    for t in range(s + 1, S):
                        xp(s, t, g).start()
                if s < S - 2:
                    for h in range(2):
                        so(0, s + 1, h, g).start()
                return 0

            lax.fori_loop(0, G, backward, 0)
            if s == 0:
                def finish(g, _):
                    for k in range(1, R):
                        src = lax.rem(row + R - k, R)
                        rc(rso.at[0, g, 0], rli.at[src // 2, src % 2, g], rl_s.at[g, k],
                           rl_r.at[g, k], sec, row).wait_recv()
                    for k in range(2):
                        v = jnp.zeros((n, rows), F32)
                        for q in range(Z):
                            v = v - rli[q, k, g].astype(F32)
                        soi[k, g] = v
                    return 0

                lax.fori_loop(0, G, finish, 0)

        rc(fs.at[0], fb.at[1 - c], fo_s, fo_r, sec, row).wait_recv()
        fwd[...] = jnp.concatenate([fb[k].reshape(N, rows).T for k in range(2)], axis=1)
        if s > 0:
            def collect(g, _):
                for k in range(2):
                    if not last:
                        rc(sob.at[0, 0, g], soi.at[k, g], so_s.at[0, g], so_r.at[k, g],
                           sec, row).wait_recv()
                if last:
                    rc(sob.at[0, 0, g], soi.at[1 - c, g], so_s.at[0, g], so_r.at[1 - c, g],
                       sec, row).wait_recv()
                return 0

            lax.fori_loop(0, G, collect, 0)
        sol[...] = jnp.concatenate([soi[k].reshape(N, rows).T for k in range(2)], axis=1)

        if s == 0:
            def drain_first(g, _):
                for k in range(1, R):
                    a0(g, k).wait_send()
                    rlc(g, k).wait_send()
                return 0

            lax.fori_loop(0, G, drain_first, 0)
        else:
            for k in range(2):
                rh(k).wait_send()
        for t in range(s + 1, S):
            ex(t).wait_send()
        fo().wait_send()

        def drain(g, _):
            if not last:
                for q in range(Z):
                    mc(s, g, q).wait_send()
                    if s > 0:
                        rsc(s, g, q).wait_send()
                for t in range(s + 2, S):
                    ps(s, t, g).wait_send()
            if s > 0:
                for t in range(min(s + 1, S - 1), S):
                    xp(s, t, g).wait_send()
            if last:
                so(0, s, 1 - c, g).wait_send()
            elif s < S - 2:
                for h in range(2):
                    so(0, s + 1, h, g).wait_send()
            return 0

        lax.fori_loop(0, G, drain, 0)

    for s in range(S):
        pl.when(sec == s)(functools.partial(section, s))


def local(rhs, coupling, diag_inverse):
    S = lax.axis_size("sec")
    R = lax.axis_size("row")
    rows, total = rhs.shape
    W = diag_inverse.shape[1]
    N = total // 2
    G = GROUPS
    n = N // G
    Z = R // 2
    half = (G, n, rows)
    vm = pltpu.VMEM
    dma = pltpu.SemaphoreType.DMA
    scratch = [
        vm((rows, total), F32),
        vm(coupling.shape, BF16),
        vm((W, W), BF16),
        vm((S, 2 * rows, W), BF16),
        vm((2,) + half, F32),
        vm((2,) + half, BF16),
        vm((2,) + half, F32),
        vm((R,) + half, BF16),
        vm((G, 2, n, rows), BF16),
        vm((S, G, 2, n, rows), BF16),
        vm((S, G, 2, n, rows), BF16),
        vm((R,) + half, F32),
        vm((2,) + half, F32),
        vm((2,) + half, F32),
        vm((2,) + half, F32),
        vm((S, G, 2, n, rows), BF16),
        vm((Z, G, 2, n, rows), BF16),
        vm((Z, G, 2, n, rows), BF16),
        vm((Z, 2) + half, BF16),
        vm((1, 2) + half, F32),
        vm((2,) + half, F32),
        dma((3,)), dma((S,)), dma((S,)),
        dma((2,)), dma((2,)),
        dma((G, R)), dma((G, R)),
        dma((G, Z)), dma((G, Z)),
        dma((S, G)), dma((S, G)),
        dma((S, G)), dma((S, G)),
        dma((G, Z)), dma((G, Z)),
        dma((G, R)), dma((G, R)),
        dma((2, G)), dma((2, G)),
        dma, dma,
    ]
    out = jax.ShapeDtypeStruct((rows, total), F32)
    block = pl.BlockSpec(memory_space=pltpu.VMEM)
    return pl.pallas_call(
        functools.partial(kernel, S, R, G),
        out_shape=(out, out),
        in_specs=[pl.BlockSpec(memory_space=pltpu.HBM)] * 3,
        out_specs=(block, block),
        scratch_shapes=scratch,
        compiler_params=pltpu.CompilerParams(
            collective_id=0, has_side_effects=True, vmem_limit_bytes=127 * 2 ** 19),
    )(rhs, coupling, diag_inverse[0])


def solution(mesh):
    return jax.shard_map(
        local,
        mesh=mesh,
        in_specs=(P(("sec", "row"), None), P(None, "row", "sec"), P("sec", None, None)),
        out_specs=(P(("sec", "row"), None), P(("sec", "row"), None)),
        check_vma=False,
    )
```
